256 devices in a mesh: ctx: 128 (over z, y, x_lo, core), head: 2 (over x_hi).
Axes of the slice: x: 4 (x_hi: 2, x_lo: 2; x = x_hi * 2 + x_lo), y: 4, z: 8, core: 2. Of those that a mesh axis runs over, the one named last changes fastest.
Arguments:
- tokens: bfloat16 [65536, 4096], P('ctx', 'head'), may hold values from -3 to 3
- gate_weight: bfloat16 [4096, 32], P('head'), may hold values from -0.04375 to 0.04375
- gate_bias: float32 [32], P('head'), may hold values from 3 to 13
- queries: bfloat16 [65536, 32, 128], P('ctx', 'head'), may hold values from -6.5 to 6.5
- key_vectors: bfloat16 [65536, 32, 128], P('ctx', 'head'), may hold values from -6.5 to 6.5
- values: bfloat16 [65536, 32, 128], P('ctx', 'head'), may hold values from -6 to 6
- pair_table: int32 [128], replicated, may hold values from 0 to 127, each once
Outputs:
- partial_out: float32 [65536, 32, 128], P('ctx', 'head')
- log_total: float32 [65536, 32], P('ctx', 'head')
The draws below stay inside these ranges and needn't reach their ends.
Inputs may be any that keep to these rules, and one draw needn't show every extreme that they name: Device p holds spans pair_table[p] and 255 - pair_table[p]; every pair once.
All inputs are finite; a program needn't handle non-finite values.
Results may differ from the reference program's by a relative error of at most 0.0025.
Values may be sent and summed in bfloat16 or wider, within the bound.
No kernel may reach another device: no remote copies, remote signals or barrier semaphores. Data moves between devices by JAX's collectives and lax.ppermute only.
A program may use at most 128 MiB of HBM per device.

```python
import jax
import jax.numpy as jnp
from jax import lax

D = 4096
HEAD_TOTAL = 32
HD = 128
TOKENS_PER_UNIT = 512
SEQ = 65536
N_CTX = 128


def gate_values(key, quick_fraction):
    gathered_keys = jax.random.split(key, 7)
    weight_matrix = jnp.clip(jax.random.normal(gathered_keys[0], (D, HEAD_TOTAL), jnp.float32), -4.0, 4.0) * (0.7 * D ** (-0.5))
    is_fast = jax.random.uniform(gathered_keys[1], (HEAD_TOTAL,)) < quick_fraction
    fast_bias = jax.random.uniform(gathered_keys[2], (HEAD_TOTAL,), minval=3.0, maxval=4.0)
    slow_bias = jax.random.uniform(gathered_keys[3], (HEAD_TOTAL,), minval=11.0, maxval=13.0)
    bias_vector = jnp.where(is_fast, fast_bias, slow_bias)
    processor_count = SEQ // TOKENS_PER_UNIT
    spike_row = jax.random.randint(gathered_keys[4], (processor_count, 1), 0, TOKENS_PER_UNIT)
    spike_head = jax.random.randint(gathered_keys[5], (processor_count,), 0, HEAD_TOTAL)
    spike_level = jax.random.uniform(gathered_keys[6], (processor_count,), minval=0.0, maxval=1.2)
    return (weight_matrix, bias_vector, spike_row, spike_head, spike_level)


def draw_tokens(key, part):
    quick_fraction = 0.5
    weight_matrix, bias_vector, spike_row, spike_head, spike_level = gate_values(key, quick_fraction)
    key = jax.random.fold_in(key, 21)
    processor_count = SEQ // TOKENS_PER_UNIT
    baseline_level = jnp.clip(jax.random.normal(key, (processor_count, TOKENS_PER_UNIT, D), jnp.float32), -3.0, 3.0)
    dispersion = D * 0.7 * D ** (-0.5) * 0.7979
    spike_scale = (bias_vector[spike_head] - spike_level) / dispersion
    motif_layout = -spike_scale[:, None] * jnp.sign(weight_matrix.T[spike_head])
    row_position = jnp.arange(TOKENS_PER_UNIT, dtype=jnp.int32)[None, :, None]
    final_output = jnp.where(row_position == spike_row[:, :, None], motif_layout[:, None, :], baseline_level)
    return final_output.reshape(SEQ, D).astype(jnp.bfloat16)


def draw_gate_weight(key, part):
    weight_matrix, bias_vector, spike_row, spike_head, spike_level = gate_values(key, 0.5)
    return weight_matrix.astype(jnp.bfloat16)


def draw_gate_bias(key, part):
    quick_fraction = 0.5
    weight_matrix, bias_vector, spike_row, spike_head, spike_level = gate_values(key, quick_fraction)
    return bias_vector.astype(jnp.float32)


def draw_queries(key, part):
    key = jax.random.fold_in(key, 11)
    baseline_level = jnp.clip(jax.random.normal(key, (SEQ, HEAD_TOTAL, HD), jnp.float32), -4.0, 4.0)
    return baseline_level.astype(jnp.bfloat16)


def draw_key_vectors(key, part):
    key = jax.random.fold_in(key, 13)
    baseline_level = jnp.clip(jax.random.normal(key, (SEQ, HEAD_TOTAL, HD), jnp.float32), -4.0, 4.0)
    return baseline_level.astype(jnp.bfloat16)


def level_of(stream_key, dims, cuts, low, top_value):
    def one(position, shards_of):
        steps = jax.random.uniform(jax.random.fold_in(jax.random.fold_in(stream_key, 6), position), (shards_of,), jnp.float32, low / len(cuts), top_value / len(cuts))
        return jnp.repeat(jnp.exp(steps), dims[position] // shards_of).reshape((-1,) + (1,) * (len(dims) - position - 1))

    gain = one(*cuts[0])
    for cut in cuts[1:]:
        gain = gain * one(*cut)
    return gain


def noise(own_key, dims, deviation, reach, shards=(), held_as=jnp.bfloat16):
    values = jax.random.normal(own_key, dims, jnp.float32) * deviation
    if len(shards) > 0:
        values = level_of(own_key, dims, shards, -0.22, 0.18) * values
    return jnp.clip(values, min=-reach, max=reach).astype(held_as)


def setup_inputs(seed: int = 0) -> dict:
    arg_keys = jax.random.split(jax.random.key(seed), 8)
    tokens = draw_tokens(jax.random.fold_in(arg_keys[7], 71), 0)
    gate_weight = draw_gate_weight(jax.random.fold_in(arg_keys[7], 71), 0)
    gate_bias = draw_gate_bias(jax.random.fold_in(arg_keys[7], 71), 0)
    queries = draw_queries(jax.random.fold_in(arg_keys[7], 71), 0)
    key_vectors = draw_key_vectors(jax.random.fold_in(arg_keys[7], 71), 0)
    values = noise(arg_keys[5], (SEQ, HEAD_TOTAL, HD), 1.0, 6.0, ((0, 128), (1, 2)))
    pair_table = jax.random.permutation(arg_keys[6], N_CTX).astype(jnp.int32)
    return {"tokens": tokens, "gate_weight": gate_weight, "gate_bias": gate_bias, "queries": queries, "key_vectors": key_vectors, "values": values, "pair_table": pair_table}


def attend(query_block, key_block, value_block, query_rows, key_rows, query_pos, key_pos, score_scale):
    visible = query_pos[:, None] >= key_pos[None, :]
    products = jnp.einsum("qhd,khd->hqk", query_block.astype(jnp.float32), key_block.astype(jnp.float32), precision=lax.Precision.HIGHEST)
    scores = products * score_scale + query_rows.T[:, :, None] - key_rows.T[:, None, :]
    row_max = jnp.max(jnp.where(visible[None], scores, -jnp.inf), axis=2)
    weights = jnp.where(visible[None], jnp.exp(scores - row_max[:, :, None]), 0.0)
    denominator = jnp.sum(weights, axis=2)
    rounded = lax.optimization_barrier(weights.astype(jnp.bfloat16)).astype(jnp.float32)
    weighted = jnp.einsum("hqk,khd->qhd", rounded, value_block.astype(jnp.float32), precision=lax.Precision.HIGHEST)
    return weighted / denominator.T[:, :, None], (row_max + jnp.log(denominator)).T


def reference(tokens, gate_weight, gate_bias, queries, key_vectors, values, pair_table):
    span_len = TOKENS_PER_UNIT // 2
    logits = jnp.dot(tokens, gate_weight, preferred_element_type=jnp.float32) + gate_bias[None, :]
    forget = lax.optimization_barrier(jax.nn.log_sigmoid(logits).astype(jnp.bfloat16)).astype(jnp.float32)
    log_rows = forget.reshape(N_CTX, 2, span_len, HEAD_TOTAL)
    totals = jnp.sum(log_rows, axis=2)
    inner = jnp.cumsum(log_rows, axis=2)
    slot_spans = jnp.stack([pair_table, 2 * N_CTX - 1 - pair_table], axis=1).astype(jnp.int32)
    by_span = jnp.zeros((2 * N_CTX, HEAD_TOTAL), jnp.float32).at[slot_spans.reshape(-1)].set(totals.reshape(2 * N_CTX, HEAD_TOTAL))
    running = jnp.cumsum(by_span, axis=0)
    offsets = jnp.concatenate([jnp.zeros((1, HEAD_TOTAL), jnp.float32), running[:-1]], axis=0)
    cumulative = (offsets[slot_spans][:, :, None, :] + inner).reshape(N_CTX, TOKENS_PER_UNIT, HEAD_TOTAL)
    within = jnp.arange(span_len, dtype=jnp.int32)
    positions = (slot_spans[:, :, None] * span_len + within[None, None, :]).reshape(N_CTX, TOKENS_PER_UNIT)
    query_dev = queries.reshape(N_CTX, TOKENS_PER_UNIT, HEAD_TOTAL, HD)
    key_dev = key_vectors.reshape(N_CTX, TOKENS_PER_UNIT, HEAD_TOTAL, HD)
    value_dev = values.reshape(N_CTX, TOKENS_PER_UNIT, HEAD_TOTAL, HD)

    def one_device(device):
        sources = [device, (device - 1) % N_CTX, (device - 2) % N_CTX]
        keys_here = jnp.concatenate([key_dev[source] for source in sources], axis=0)
        values_here = jnp.concatenate([value_dev[source] for source in sources], axis=0)
        rows_here = jnp.concatenate([cumulative[source] for source in sources], axis=0)
        pos_here = jnp.concatenate([positions[source] for source in sources], axis=0)
        return attend(query_dev[device], keys_here, values_here, cumulative[device], rows_here, positions[device], pos_here, HD ** -0.5)

    outputs, log_sums = lax.map(one_device, jnp.arange(N_CTX, dtype=jnp.int32))
    return outputs.reshape(SEQ, HEAD_TOTAL, HD), log_sums.reshape(SEQ, HEAD_TOTAL)
```

```python
import functools

import jax
import jax.numpy as jnp
from jax import lax
from jax.experimental import pallas as pl
from jax.experimental.pallas import tpu as pltpu
from jax.sharding import PartitionSpec as P

VMEM_LIMIT = 48 * 1024 * 1024
CHUNK = 4
HALF = 256


def gate_kernel(tok_ref, w_ref, keep_ref, send_ref):
    logits = lax.dot_general(
        w_ref[...], tok_ref[...], (((0,), (1,)), ((), ())), preferred_element_type=jnp.float32
    )
    heads = keep_ref.shape[0]
    first = lax.axis_index("head") == 0
    low, high = logits[:heads], logits[heads:]
    keep_ref[...] = jnp.where(first, low, high)
    send_ref[...] = jnp.where(first, high, low)


def gate_logits(tokens, gate_weight):
    rows, depth = tokens.shape
    heads = gate_weight.shape[1] // 2
    step = 128
    out = jax.ShapeDtypeStruct((heads, rows), jnp.float32)
    return pl.pallas_call(
        gate_kernel,
        grid=(rows // step,),
        in_specs=[
            pl.BlockSpec((step, depth), lambda i: (i, 0)),
            pl.BlockSpec(gate_weight.shape, lambda i: (0, 0)),
        ],
        out_specs=[pl.BlockSpec((heads, step), lambda i: (0, i))] * 2,
        out_shape=[out, out],
        compiler_params=pltpu.CompilerParams(vmem_limit_bytes=VMEM_LIMIT),
        name="gate_logits",
    )(tokens, gate_weight)


def heads_first_kernel(*refs, n_in):
    ins, outs, wide = refs[:n_in], refs[n_in:-1], refs[-1]
    rows, heads, size = ins[0].shape
    for which, ref in enumerate(ins):
        wide[...] = ref[...].reshape(rows * heads, size).astype(jnp.float32)
        for h in range(heads):
            one = wide[pl.ds(h, rows, stride=heads), :].astype(jnp.bfloat16)
            outs[h // CHUNK][h % CHUNK, which] = one


def heads_first(*arrays):
    rows, heads, size = arrays[0].shape
    step = 64
    n_in = len(arrays)
    n_out = heads // CHUNK
    out = jax.ShapeDtypeStruct((CHUNK, n_in, rows, size), jnp.bfloat16)
    return pl.pallas_call(
        functools.partial(heads_first_kernel, n_in=n_in),
        grid=(rows // step,),
        in_specs=[pl.BlockSpec((step, heads, size), lambda i: (i, 0, 0))] * n_in,
        out_specs=[pl.BlockSpec((CHUNK, n_in, step, size), lambda i: (0, 0, i, 0))] * n_out,
        out_shape=[out] * n_out,
        scratch_shapes=[pltpu.VMEM((step * heads, size), jnp.float32)],
        compiler_params=pltpu.CompilerParams(vmem_limit_bytes=VMEM_LIMIT),
        name="heads_first",
    )(*arrays)


def forget_kernel(pair_ref, keep_ref, recv_ref, bias_ref, inner_ref, spread_ref):
    device = lax.axis_index("ctx")
    n_span = 2 * pair_ref.shape[0]
    logits = keep_ref[...] + recv_ref[...] + bias_ref[...]
    forget = (jnp.minimum(logits, 0.0) - jnp.log1p(jnp.exp(-jnp.abs(logits)))).astype(jnp.bfloat16)
    row = lax.broadcasted_iota(jnp.int32, (HALF, HALF), 0)
    col = lax.broadcasted_iota(jnp.int32, (HALF, HALF), 1)
    upto = (row <= col).astype(jnp.float32).astype(jnp.bfloat16)
    low = jnp.dot(forget[:, :HALF], upto, preferred_element_type=jnp.float32)
    high = jnp.dot(forget[:, HALF:], upto, preferred_element_type=jnp.float32)
    inner_ref[:, :HALF] = low
    inner_ref[:, HALF:] = high
    span = pair_ref[device]
    lane = lax.broadcasted_iota(jnp.int32, spread_ref.shape, 1)
    spread_ref[...] = jnp.where(lane == span, low[:, HALF - 1 :], 0.0) + jnp.where(
        lane == n_span - 1 - span, high[:, HALF - 1 :], 0.0
    )


def forget_rows(pair_table, keep, recv, bias):
    heads, rows = keep.shape
    n_span = 2 * pair_table.shape[0]
    whole = pl.BlockSpec(memory_space=pltpu.VMEM)
    return pl.pallas_call(
        forget_kernel,
        in_specs=[pl.BlockSpec(memory_space=pltpu.SMEM), whole, whole, whole],
        out_specs=[whole, whole],
        out_shape=[
            jax.ShapeDtypeStruct((heads, rows), jnp.float32),
            jax.ShapeDtypeStruct((heads, n_span), jnp.float32),
        ],
        compiler_params=pltpu.CompilerParams(vmem_limit_bytes=VMEM_LIMIT),
        name="forget_rows",
    )(pair_table, keep, recv, bias)


def offsets_kernel(pair_ref, by_span_ref, own_ref, near_ref, far_ref, cum_ref):
    n_ctx = pair_ref.shape[0]
    device = lax.axis_index("ctx")
    by_span = by_span_ref[...]
    lane = lax.broadcasted_iota(jnp.int32, by_span.shape, 1)
    for distance, ref in enumerate((own_ref, near_ref, far_ref)):
        span = pair_ref[lax.rem(device + n_ctx - distance, n_ctx)]
        for s, c in enumerate((span, 2 * n_ctx - 1 - span)):
            offset = jnp.sum(jnp.where(lane < c, by_span, 0.0), axis=1, keepdims=True)
            part = slice(s * HALF, (s + 1) * HALF)
            cum_ref[:, distance, part] = ref[:, part] + offset


def offsets(pair_table, by_span, own, near, far):
    heads, rows = own.shape
    whole = pl.BlockSpec(memory_space=pltpu.VMEM)
    return pl.pallas_call(
        offsets_kernel,
        in_specs=[pl.BlockSpec(memory_space=pltpu.SMEM), whole, whole, whole, whole],
        out_specs=whole,
        out_shape=jax.ShapeDtypeStruct((heads, 3, rows), jnp.float32),
        compiler_params=pltpu.CompilerParams(vmem_limit_bytes=VMEM_LIMIT),
        name="offsets",
    )(pair_table, by_span, own, near, far)


def attend_kernel(pair_ref, q_ref, own_ref, near_ref, far_ref, cum_ref, *rest, scale, sub):
    out_ref, log_ref = rest[-2:]
    flat = out_ref.reshape(out_ref.shape[0] * out_ref.shape[2], out_ref.shape[3])
    n_ctx = pair_ref.shape[0]
    device = lax.axis_index("ctx")
    span = pair_ref[device]
    near_lower = span > pair_ref[lax.rem(device + n_ctx - 1, n_ctx)]
    far_lower = span > pair_ref[lax.rem(device + n_ctx - 2, n_ctx)]
    if len(rest) > 2:
        out_ref[...] = rest[0][...]
    row = lax.broadcasted_iota(jnp.int32, (HALF, HALF), 0)
    col = lax.broadcasted_iota(jnp.int32, (HALF, HALF), 1)
    tri = row >= col
    sources = (own_ref, near_ref, far_ref)

    def one_half(h, s, pieces):
        q = q_ref[h, 0, s * HALF : (s + 1) * HALF, :]
        scores = []
        for source, half, masked in pieces:
            part = slice(half * HALF, (half + 1) * HALF)
            prod = lax.dot_general(
                q, sources[source][h, 0, part, :], (((1,), (1,)), ((), ())),
                preferred_element_type=jnp.float32,
            )
            sc = prod * scale - cum_ref[h, source : source + 1, part]
            scores.append(jnp.where(tri, sc, -jnp.inf) if masked else sc)
        top = functools.reduce(jnp.maximum, scores)
        top = jnp.max(top, axis=1, keepdims=True)
        total = None
        acc = None
        for sc, (source, half, _) in zip(scores, pieces):
            part = slice(half * HALF, (half + 1) * HALF)
            w = jnp.exp(sc - top)
            total = w if total is None else total + w
            o = jnp.dot(
                w.astype(jnp.bfloat16), sources[source][h, 1, part, :],
                preferred_element_type=jnp.float32,
            )
            acc = o if acc is None else acc + o
        total = jnp.sum(total, axis=1, keepdims=True)
        flat[pl.ds(s * HALF * 8 + sub + h, HALF, stride=8), :] = acc / total
        log_ref[h, s * HALF : (s + 1) * HALF, :] = top + jnp.log(total)

    for near_is in (False, True):
        for far_is in (False, True):
            lower = [(0, 0, True)]
            upper = [(0, 0, False), (0, 1, True), (1, 0, False), (2, 0, False)]
            (lower if near_is else upper).append((1, 0 if near_is else 1, False))
            (lower if far_is else upper).append((2, 0 if far_is else 1, False))

            @pl.when((near_lower == near_is) & (far_lower == far_is))
            def _(lower=lower, upper=upper):
                @pl.loop(0, q_ref.shape[0])
                def _(h):
                    one_half(h, 0, lower)
                    one_half(h, 1, upper)


def attend(index, pair_table, q, own, near, far, cum, previous):
    heads, _, rows = cum.shape
    size = q.shape[-1]
    group = index * CHUNK // 8
    sub = index * CHUNK % 8
    whole = pl.BlockSpec(own.shape, lambda i: (0, 0, 0, 0))
    block = pl.BlockSpec((rows, 1, 8, size), lambda i: (0, group, 0, 0))
    out = jax.ShapeDtypeStruct((rows, heads // 8, 8, size), jnp.float32)
    in_specs = [
        pl.BlockSpec(memory_space=pltpu.SMEM),
        pl.BlockSpec(q.shape, lambda i: (0, 0, 0, 0)),
        whole,
        whole,
        whole,
        pl.BlockSpec((CHUNK, 3, rows), lambda i: (index, 0, 0)),
    ]
    args = [pair_table, q, own, near, far, cum]
    aliases = {}
    if previous is not None:
        in_specs.append(block if sub else pl.BlockSpec(memory_space=pl.ANY))
        args.append(previous)
        aliases = {6: 0}
    kernel = attend_kernel
    return pl.pallas_call(
        functools.partial(kernel, scale=size**-0.5, sub=sub) if sub or previous is None
        else functools.partial(skip_previous, scale=size**-0.5, sub=sub),
        grid=(1,),
        in_specs=in_specs,
        out_specs=[block, pl.BlockSpec((CHUNK, rows, 1), lambda i: (0, 0, 0))],
        out_shape=[out, jax.ShapeDtypeStruct((CHUNK, rows, 1), jnp.float32)],
        input_output_aliases=aliases,
        compiler_params=pltpu.CompilerParams(vmem_limit_bytes=VMEM_LIMIT),
        name="attend",
    )(*args)


def skip_previous(*refs, scale, sub):
    attend_kernel(*refs[:6], *refs[7:], scale=scale, sub=sub)


def shards(tokens, gate_weight, gate_bias, queries, key_vectors, values, pair_table):
    rows, heads, size = queries.shape
    n_ctx = lax.axis_size("ctx")
    even = lax.rem(lax.axis_index("ctx"), 2) == 0
    all_pairs = [(i, (i + 1) % n_ctx) for i in range(n_ctx)]
    two_pairs = [(i, (i + 2) % n_ctx) for i in range(n_ctx)]
    even_two = [(i, (i + 2) % n_ctx) for i in range(0, n_ctx, 2)]
    even_one = [(i, i + 1) for i in range(0, n_ctx, 2)]

    keep, send = gate_logits(tokens, gate_weight)
    recv = lax.ppermute(send, "head", [(0, 1), (1, 0)])
    own = heads_first(key_vectors, values)
    inner, spread = forget_rows(pair_table, keep, recv, gate_bias[:, None])
    n_chunk = heads // CHUNK
    near = [None] * n_chunk
    direct = [None] * n_chunk
    near[0] = lax.ppermute(own[0], "ctx", all_pairs)
    direct[0] = lax.ppermute(own[0], "ctx", even_two)
    by_span = spread
    by_span = by_span + lax.ppermute(by_span, "ctx", [(i, i ^ 2) for i in range(n_ctx)])
    near_inner = lax.ppermute(inner, "ctx", all_pairs)
    far_inner = lax.ppermute(inner, "ctx", two_pairs)
    later, by_span, near_inner, far_inner = lax.optimization_barrier(
        (own[1:], by_span, near_inner, far_inner)
    )
    own = [own[0], *later]
    for c in range(1, n_chunk):
        near[c] = lax.ppermute(own[c], "ctx", all_pairs)
        direct[c] = lax.ppermute(own[c], "ctx", even_two)
    for bit in (1, 4, 8, 16, 32, 64):
        by_span = by_span + lax.ppermute(by_span, "ctx", [(i, i ^ bit) for i in range(n_ctx)])
    cum = offsets(pair_table, by_span, inner, near_inner, far_inner)
    q = heads_first(queries)
    out = None
    logs = []
    for c in range(n_chunk):
        passed = lax.ppermute(near[c], "ctx", even_one)
        far = jnp.where(even, direct[c], passed)
        out, log = attend(c, pair_table, q[c], own[c], near[c], far, cum, out)
        logs.append(log[:, :, 0])
    log_total = jnp.concatenate(logs, axis=0).T + cum[:, 0, :].T
    return out.reshape(rows, heads, size), log_total


def solution(mesh):
    return jax.shard_map(
        shards,
        mesh=mesh,
        in_specs=(
            P("ctx", "head"),
            P("head", None),
            P("head"),
            P("ctx", "head", None),
            P("ctx", "head", None),
            P("ctx", "head", None),
            P(),
        ),
        out_specs=(P("ctx", "head", None), P("ctx", "head")),
        check_vma=False,
    )
```

```python
import functools
import math

import jax
import jax.numpy as jnp
from jax import lax
from jax.experimental import pallas as pl
from jax.experimental.pallas import tpu as pltpu
from jax.sharding import PartitionSpec as P

VMEM_LIMIT = 24 * 1024 * 1024
HALF = 256
SIZES = (1, 4, 4, 4, 3)
GROUPS = ((0,), (1, 2), (3,), (4,))
LOG2E = math.log2(math.e)


SMALL = pl.CostEstimate(flops=1, bytes_accessed=1, transcendentals=0)


def gate_kernel(tok_ref, w_ref, keep_ref, send_ref):
    logits = lax.dot_general(
        tok_ref[...], w_ref[...], (((1,), (1,)), ((), ())), preferred_element_type=jnp.float32
    )
    logits = jnp.transpose(logits)
    heads = keep_ref.shape[0]
    first = lax.axis_index("head") == 0
    low, high = logits[:heads], logits[heads:]
    keep_ref[...] = jnp.where(first, low, high)
    send_ref[...] = jnp.where(first, high, low)


def gate_logits(tokens, gate_weight):
    rows, depth = tokens.shape
    heads = gate_weight.shape[0] // 2
    step = 256
    out = jax.ShapeDtypeStruct((heads, rows), jnp.float32)
    return pl.pallas_call(
        gate_kernel,
        grid=(rows // step,),
        in_specs=[
            pl.BlockSpec((step, depth), lambda i: (i, 0)),
            pl.BlockSpec(gate_weight.shape, lambda i: (0, 0)),
        ],
        out_specs=[pl.BlockSpec((heads, step), lambda i: (0, i))] * 2,
        out_shape=[out, out],
        compiler_params=pltpu.CompilerParams(vmem_limit_bytes=VMEM_LIMIT),
        cost_estimate=SMALL,
        name="gate_logits",
    )(tokens, gate_weight)


def heads_first_kernel(*refs, n_in, sizes):
    ins, outs = refs[:n_in], refs[n_in:]
    for which, ref in enumerate(ins):
        turned = jnp.swapaxes(ref[...], 0, 1)
        first = 0
        for out, n in zip(outs, sizes):
            out[:, which] = turned[first : first + n]
            first += n


def heads_first(sizes, *arrays):
    rows, heads, size = arrays[0].shape
    step = 128
    n_in = len(arrays)
    return pl.pallas_call(
        functools.partial(heads_first_kernel, n_in=n_in, sizes=sizes),
        grid=(rows // step,),
        in_specs=[pl.BlockSpec((step, heads, size), lambda i: (i, 0, 0))] * n_in,
        out_specs=[pl.BlockSpec((n, n_in, step, size), lambda i: (0, 0, i, 0)) for n in sizes],
        out_shape=[jax.ShapeDtypeStruct((n, n_in, rows, size), jnp.bfloat16) for n in sizes],
        compiler_params=pltpu.CompilerParams(vmem_limit_bytes=VMEM_LIMIT),
        cost_estimate=SMALL,
        name="heads_first",
    )(*arrays)


def forget_kernel(pair_ref, keep_ref, recv_ref, bias_ref, inner_ref, spread_ref):
    device = lax.axis_index("ctx")
    n_span = 2 * pair_ref.shape[0]
    line = lax.broadcasted_iota(jnp.int32, keep_ref.shape, 0)
    bias = jnp.zeros(keep_ref.shape, jnp.float32)
    for h in range(keep_ref.shape[0]):
        bias = jnp.where(line == h, bias_ref[h], bias)
    logits = keep_ref[...] + recv_ref[...] + bias
    forget = (jnp.minimum(logits, 0.0) - jnp.log1p(jnp.exp(-jnp.abs(logits)))).astype(jnp.bfloat16)
    row = lax.broadcasted_iota(jnp.int32, (HALF, HALF), 0)
    col = lax.broadcasted_iota(jnp.int32, (HALF, HALF), 1)
    upto = (row <= col).astype(jnp.float32).astype(jnp.bfloat16)
    low = jnp.dot(forget[:, :HALF], upto, preferred_element_type=jnp.float32)
    high = jnp.dot(forget[:, HALF:], upto, preferred_element_type=jnp.float32)
    inner_ref[:, :HALF] = low
    inner_ref[:, HALF:] = high
    span = pair_ref[device]
    lane = lax.broadcasted_iota(jnp.int32, spread_ref.shape, 1)
    spread_ref[...] = jnp.where(lane == span, low[:, HALF - 1 :], 0.0) + jnp.where(
        lane == n_span - 1 - span, high[:, HALF - 1 :], 0.0
    )


def forget_rows(pair_table, keep, recv, bias):
    heads, rows = keep.shape
    n_span = 2 * pair_table.shape[0]
    whole = pl.BlockSpec(memory_space=pltpu.VMEM)
    return pl.pallas_call(
        forget_kernel,
        in_specs=[
            pl.BlockSpec(memory_space=pltpu.SMEM),
            whole,
            whole,
            pl.BlockSpec(memory_space=pltpu.SMEM),
        ],
        out_specs=[whole, whole],
        out_shape=[
            jax.ShapeDtypeStruct((heads, rows), jnp.float32),
            jax.ShapeDtypeStruct((heads, n_span), jnp.float32),
        ],
        compiler_params=pltpu.CompilerParams(vmem_limit_bytes=VMEM_LIMIT),
        cost_estimate=SMALL,
        name="forget_rows",
    )(pair_table, keep, recv, bias)


def offsets_kernel(pair_ref, by_span_ref, own_ref, near_ref, far_ref, cum_ref):
    n_ctx = pair_ref.shape[0]
    device = lax.axis_index("ctx")
    by_span = by_span_ref[...]
    lane = lax.broadcasted_iota(jnp.int32, by_span.shape, 1)
    for distance, ref in enumerate((own_ref, near_ref, far_ref)):
        span = pair_ref[lax.rem(device + n_ctx - distance, n_ctx)]
        for s, c in enumerate((span, 2 * n_ctx - 1 - span)):
            offset = jnp.sum(jnp.where(lane < c, by_span, 0.0), axis=1, keepdims=True)
            part = slice(s * HALF, (s + 1) * HALF)
            cum_ref[distance, :, part] = ref[:, part] + offset


def offsets(pair_table, by_span, own, near, far):
    heads, rows = own.shape
    whole = pl.BlockSpec(memory_space=pltpu.VMEM)
    return pl.pallas_call(
        offsets_kernel,
        in_specs=[pl.BlockSpec(memory_space=pltpu.SMEM), whole, whole, whole, whole],
        out_specs=whole,
        out_shape=jax.ShapeDtypeStruct((3, heads, rows), jnp.float32),
        compiler_params=pltpu.CompilerParams(vmem_limit_bytes=VMEM_LIMIT),
        cost_estimate=SMALL,
        name="offsets",
    )(pair_table, by_span, own, near, far)


def attend_kernel(pair_ref, q_ref, cum_ref, *rest, parts, held, scale):
    n_part = len(parts)
    own, crossed, beside, far = (rest[i * n_part : (i + 1) * n_part] for i in range(4))
    out_any, log_ref, near_ref, bias_ref, side_ref, done_ref, in_sems, out_sems = rest[-8:]
    n_ctx = pair_ref.shape[0]
    n, _, rows, size = near_ref.shape
    first = parts[0][0]
    device = lax.axis_index("ctx")
    even = lax.rem(device, 2) == 0
    span = pair_ref[device]
    near_lower = span > pair_ref[lax.rem(device + n_ctx - 1, n_ctx)]
    far_lower = span > pair_ref[lax.rem(device + n_ctx - 2, n_ctx)]

    def store(j, slot):
        return pltpu.make_async_copy(
            done_ref.at[slot], out_any.at[:, first + j, :], out_sems.at[slot]
        )

    for part, (start, count) in enumerate(parts):
        here = pl.ds(start - first, count)

        @pl.when(even)
        def _(part=part, here=here):
            pltpu.make_async_copy(crossed[part], near_ref.at[here], in_sems.at[part]).start()

        @pl.when(jnp.logical_not(even))
        def _(part=part, here=here):
            pltpu.make_async_copy(beside[part], near_ref.at[here], in_sems.at[part]).start()

    side_ref[...] = jnp.zeros_like(side_ref)
    for j in range(n):
        for d in range(3):
            bias_ref[j, d] = cum_ref[d, first + j : first + j + 1, :] * LOG2E
    if held:
        log_ref[...] = rest[4 * n_part + 1][...]

    def one_half(part, k, h, slot, s, pieces):
        sources = (own[part].at[k], near_ref.at[h], far[part].at[k])
        mine = pl.ds(s * HALF, HALF)
        q = q_ref[first + h, 0, mine, :]
        scores = []
        for source, half, masked in pieces:
            block = slice(half * HALF, (half + 1) * HALF)
            prod = lax.dot_general(
                q, sources[source][0, block, :], (((1,), (1,)), ((), ())),
                preferred_element_type=jnp.float32,
            )
            sc = prod * (scale * LOG2E) - bias_ref[h, source, :, block]
            if masked:
                row = lax.broadcasted_iota(jnp.int32, (HALF, HALF), 0)
                col = lax.broadcasted_iota(jnp.int32, (HALF, HALF), 1)
                sc = jnp.where(row >= col, sc, -jnp.inf)
            scores.append(sc)
        top = jnp.max(functools.reduce(jnp.maximum, scores), axis=1, keepdims=True)
        total = acc = None
        for sc, (source, half, _) in zip(scores, pieces):
            block = slice(half * HALF, (half + 1) * HALF)
            w = jnp.exp2(sc - top)
            total = w if total is None else total + w
            o = jnp.dot(
                w.astype(jnp.bfloat16), sources[source][1, block, :],
                preferred_element_type=jnp.float32,
            )
            acc = o if acc is None else acc + o
        total = jnp.sum(total, axis=1, keepdims=True)
        done_ref[slot, mine, :] = acc / total
        lane = lax.broadcasted_iota(jnp.int32, (HALF, size), 1)
        side_ref[mine, :] = jnp.where(lane == h, top + jnp.log2(total), side_ref[mine, :])

    for part, (start, count) in enumerate(parts):
        here = pl.ds(start - first, count)
        pltpu.make_async_copy(crossed[part], near_ref.at[here], in_sems.at[part]).wait()

    for near_is in (False, True):
        for far_is in (False, True):
            lower = [(0, 0, True)]
            upper = [(0, 0, False), (0, 1, True), (1, 0, False), (2, 0, False)]
            (lower if near_is else upper).append((1, 0 if near_is else 1, False))
            (lower if far_is else upper).append((2, 0 if far_is else 1, False))

            @pl.when((near_lower == near_is) & (far_lower == far_is))
            def _(lower=lower, upper=upper):
                for part, (start, count) in enumerate(parts):
                    base = start - first

                    @pl.loop(0, count)
                    def _(k, part=part, base=base):
                        h = base + k
                        slot = lax.rem(h, 2)

                        @pl.when(h >= 2)
                        def _():
                            store(h - 2, slot).wait()

                        one_half(part, k, h, slot, 0, lower)
                        one_half(part, k, h, slot, 1, upper)
                        store(h, slot).start()

    logs = jnp.transpose(side_ref[...])[:n] * (1.0 / LOG2E)
    log_ref[first : first + n, :] = logs + cum_ref[0, first : first + n, :]
    for j in range(max(0, n - 2), n):
        store(j, j % 2).wait()


def attend(parts, pair_table, q, cum, own, crossed, beside, far, previous):
    _, _, rows, size = q.shape
    heads = cum.shape[1]
    n = sum(count for _, count in parts)
    there = pl.BlockSpec(memory_space=pl.ANY)
    whole = pl.BlockSpec(memory_space=pltpu.VMEM)
    args = [pair_table, q, cum, *own, *crossed, *beside, *far]
    in_specs = [pl.BlockSpec(memory_space=pltpu.SMEM)] + [whole] * (2 + 4 * len(parts))
    aliases = {}
    if previous is not None:
        aliases = {len(args): 0, len(args) + 1: 1}
        in_specs += [there, whole]
        args += list(previous)
    return pl.pallas_call(
        functools.partial(
            attend_kernel, parts=parts, held=previous is not None, scale=size**-0.5
        ),
        in_specs=in_specs,
        out_specs=[there, whole],
        out_shape=[
            jax.ShapeDtypeStruct((rows, heads, size), jnp.float32),
            jax.ShapeDtypeStruct((heads, rows), jnp.float32),
        ],
        scratch_shapes=[
            pltpu.VMEM((n, 2, rows, size), jnp.bfloat16),
            pltpu.VMEM((n, 3, 1, rows), jnp.float32),
            pltpu.VMEM((rows, size), jnp.float32),
            pltpu.VMEM((2, rows, size), jnp.float32),
            pltpu.SemaphoreType.DMA((len(parts),)),
            pltpu.SemaphoreType.DMA((2,)),
        ],
        input_output_aliases=aliases,
        compiler_params=pltpu.CompilerParams(vmem_limit_bytes=VMEM_LIMIT),
        cost_estimate=SMALL,
        name="attend",
    )(*args)


def summed_over_ctx(x):
    n_ctx = lax.axis_size("ctx")
    core, column, row, layer = 1, 2, 4, 16

    def behind(x, stride, size, by):
        pairs = []
        for i in range(n_ctx):
            at = i // stride % size
            pairs.append((i, i + ((at - by) % size - at) * stride))
        return lax.ppermute(x, "ctx", pairs)

    both = [(i, i ^ core) for i in range(n_ctx)]
    side = [(i, i ^ column) for i in range(n_ctx)]
    across = [(i, i ^ core ^ column) for i in range(n_ctx)]
    x = x + lax.ppermute(x, "ctx", both) + lax.ppermute(x, "ctx", side) + lax.ppermute(x, "ctx", across)
    x = yield x
    passing = x
    for _ in range(3):
        passing = behind(passing, row, 4, 1)
        x = x + passing
    x = x + behind(x, layer, 8, 1)
    x = x + behind(x, layer, 8, 2)
    passing = behind(behind(x, layer, 8, 2), layer, 8, 2)
    yield x + passing


def shards(tokens, gate_weight, gate_bias, queries, key_vectors, values, pair_table):
    n_ctx = lax.axis_size("ctx")
    next_chip = [(i, (i + (1 if i % 2 else 3)) % n_ctx) for i in range(n_ctx)]
    even_to_odd = [(i, i + 1) for i in range(0, n_ctx, 2)]
    swap = [(i, i ^ 1) for i in range(n_ctx)]
    n_chunk = len(SIZES)

    keep, send = gate_logits(tokens, gate_weight.T)
    recv = lax.ppermute(send, "head", [(0, 1), (1, 0)])
    key_vectors, values, keep = lax.optimization_barrier((key_vectors, values, keep))
    own = heads_first(SIZES, key_vectors, values)
    crossed = [lax.ppermute(own[0], "ctx", next_chip)]
    keep, *own = lax.optimization_barrier((keep, *own))
    inner, spread = forget_rows(pair_table, keep, recv, gate_bias)
    steps = summed_over_ctx(spread)
    on_plane = next(steps)
    crossed_inner = lax.ppermute(inner, "ctx", next_chip)
    crossed[0], *own, on_plane, crossed_inner = lax.optimization_barrier(
        (crossed[0], *own, on_plane, crossed_inner)
    )
    for c in range(1, n_chunk):
        crossed.append(lax.ppermute(own[c], "ctx", next_chip))
    beside_inner = lax.ppermute(inner, "ctx", even_to_odd)
    far_inner = lax.ppermute(crossed_inner, "ctx", swap)
    even = lax.rem(lax.axis_index("ctx"), 2) == 0
    near_inner = jnp.where(even, crossed_inner, beside_inner)
    queries, on_plane = lax.optimization_barrier((queries, on_plane))
    (q,) = heads_first((queries.shape[1],), queries)
    q, on_plane = lax.optimization_barrier((q, on_plane))
    by_span = steps.send(on_plane)
    cum = offsets(pair_table, by_span, inner, near_inner, far_inner)
    starts = [sum(SIZES[:c]) for c in range(n_chunk)]
    beside = [None] * n_chunk
    far = [None] * n_chunk
    results = earlier = None
    for group in GROUPS:
        for c in group:
            gate = earlier if group == GROUPS[-1] else results
            mine, gate = lax.optimization_barrier((own[c], gate))
            beside[c] = lax.ppermute(mine, "ctx", even_to_odd)
            across, results = lax.optimization_barrier((crossed[c], results))
            far[c] = lax.ppermute(across, "ctx", swap)
        earlier = results
        results = attend(
            tuple((starts[c], SIZES[c]) for c in group), pair_table, q, cum,
            [own[c] for c in group], [crossed[c] for c in group],
            [beside[c] for c in group], [far[c] for c in group], results,
        )
    out, log_total = results
    return out, log_total.T


def solution(mesh):
    return jax.shard_map(
        shards,
        mesh=mesh,
        in_specs=(
            P("ctx", "head"),
            P("head", None),
            P("head"),
            P("ctx", "head", None),
            P("ctx", "head", None),
            P("ctx", "head", None),
            P(),
        ),
        out_specs=(P("ctx", "head", None), P("ctx", "head")),
        check_vma=False,
    )
```

```python
import functools
import math

import jax
import jax.numpy as jnp
from jax import lax
from jax.experimental import pallas as pl
from jax.experimental.pallas import tpu as pltpu
from jax.sharding import PartitionSpec as P

VMEM_LIMIT = 24 * 1024 * 1024
HALF = 256
SIZES = (1, 4, 4, 5, 2)
GROUPS = ((0,), (1, 2), (3,), (4,))
LOG2E = math.log2(math.e)


SMALL = pl.CostEstimate(flops=1, bytes_accessed=1, transcendentals=0)


def gate_kernel(tok_ref, w_ref, keep_ref, send_ref):
    logits = lax.dot_general(
        tok_ref[...], w_ref[...], (((1,), (1,)), ((), ())), preferred_element_type=jnp.float32
    )
    logits = jnp.transpose(logits)
    heads = keep_ref.shape[0]
    first = lax.axis_index("head") == 0
    low, high = logits[:heads], logits[heads:]
    keep_ref[...] = jnp.where(first, low, high)
    send_ref[...] = jnp.where(first, high, low)


def gate_logits(tokens, gate_weight):
    rows, depth = tokens.shape
    heads = gate_weight.shape[0] // 2
    step = 256
    out = jax.ShapeDtypeStruct((heads, rows), jnp.float32)
    return pl.pallas_call(
        gate_kernel,
        grid=(rows // step,),
        in_specs=[
            pl.BlockSpec((step, depth), lambda i: (i, 0)),
            pl.BlockSpec(gate_weight.shape, lambda i: (0, 0)),
        ],
        out_specs=[pl.BlockSpec((heads, step), lambda i: (0, i))] * 2,
        out_shape=[out, out],
        compiler_params=pltpu.CompilerParams(vmem_limit_bytes=VMEM_LIMIT),
        cost_estimate=SMALL,
        name="gate_logits",
    )(tokens, gate_weight)


def heads_first_kernel(*refs, n_in, sizes):
    ins, outs = refs[:n_in], refs[-len(sizes) :]
    for which, ref in enumerate(ins):
        turned = jnp.swapaxes(ref[...], 0, 1)
        first = 0
        for out, n in zip(outs, sizes):
            out[:, which] = turned[first : first + n]
            first += n


def heads_first(sizes, *arrays, after=()):
    rows, heads, size = arrays[0].shape
    step = 128
    n_in = len(arrays)
    return pl.pallas_call(
        functools.partial(heads_first_kernel, n_in=n_in, sizes=sizes),
        grid=(rows // step,),
        in_specs=[pl.BlockSpec((step, heads, size), lambda i: (i, 0, 0))] * n_in
        + [pl.BlockSpec(memory_space=pl.ANY)] * len(after),
        out_specs=[pl.BlockSpec((n, n_in, step, size), lambda i: (0, 0, i, 0)) for n in sizes],
        out_shape=[jax.ShapeDtypeStruct((n, n_in, rows, size), jnp.bfloat16) for n in sizes],
        compiler_params=pltpu.CompilerParams(vmem_limit_bytes=VMEM_LIMIT),
        cost_estimate=SMALL,
        name="heads_first",
    )(*arrays, *after)


def forget_kernel(pair_ref, keep_ref, recv_ref, bias_ref, inner_ref, spread_ref):
    device = lax.axis_index("ctx")
    n_span = 2 * pair_ref.shape[0]
    line = lax.broadcasted_iota(jnp.int32, keep_ref.shape, 0)
    bias = jnp.zeros(keep_ref.shape, jnp.float32)
    for h in range(keep_ref.shape[0]):
        bias = jnp.where(line == h, bias_ref[h], bias)
    logits = keep_ref[...] + recv_ref[...] + bias
    forget = (jnp.minimum(logits, 0.0) - jnp.log1p(jnp.exp(-jnp.abs(logits)))).astype(jnp.bfloat16)
    row = lax.broadcasted_iota(jnp.int32, (HALF, HALF), 0)
    col = lax.broadcasted_iota(jnp.int32, (HALF, HALF), 1)
    upto = (row <= col).astype(jnp.float32).astype(jnp.bfloat16)
    low = jnp.dot(forget[:, :HALF], upto, preferred_element_type=jnp.float32)
    high = jnp.dot(forget[:, HALF:], upto, preferred_element_type=jnp.float32)
    inner_ref[:, :HALF] = low
    inner_ref[:, HALF:] = high
    span = pair_ref[device]
    lane = lax.broadcasted_iota(jnp.int32, spread_ref.shape, 1)
    spread_ref[...] = jnp.where(lane == span, low[:, HALF - 1 :], 0.0) + jnp.where(
        lane == n_span - 1 - span, high[:, HALF - 1 :], 0.0
    )


def forget_rows(pair_table, keep, recv, bias):
    heads, rows = keep.shape
    n_span = 2 * pair_table.shape[0]
    whole = pl.BlockSpec(memory_space=pltpu.VMEM)
    return pl.pallas_call(
        forget_kernel,
        in_specs=[
            pl.BlockSpec(memory_space=pltpu.SMEM),
            whole,
            whole,
            pl.BlockSpec(memory_space=pltpu.SMEM),
        ],
        out_specs=[whole, whole],
        out_shape=[
            jax.ShapeDtypeStruct((heads, rows), jnp.float32),
            jax.ShapeDtypeStruct((heads, n_span), jnp.float32),
        ],
        compiler_params=pltpu.CompilerParams(vmem_limit_bytes=VMEM_LIMIT),
        cost_estimate=SMALL,
        name="forget_rows",
    )(pair_table, keep, recv, bias)


def offsets_kernel(pair_ref, by_span_ref, own_ref, near_ref, far_ref, cum_ref):
    n_ctx = pair_ref.shape[0]
    device = lax.axis_index("ctx")
    by_span = by_span_ref[...]
    lane = lax.broadcasted_iota(jnp.int32, by_span.shape, 1)
    for distance, ref in enumerate((own_ref, near_ref, far_ref)):
        span = pair_ref[lax.rem(device + n_ctx - distance, n_ctx)]
        for s, c in enumerate((span, 2 * n_ctx - 1 - span)):
            offset = jnp.sum(jnp.where(lane < c, by_span, 0.0), axis=1, keepdims=True)
            part = slice(s * HALF, (s + 1) * HALF)
            cum_ref[distance, :, part] = ref[:, part] + offset


def offsets(pair_table, by_span, own, near, far):
    heads, rows = own.shape
    whole = pl.BlockSpec(memory_space=pltpu.VMEM)
    return pl.pallas_call(
        offsets_kernel,
        in_specs=[pl.BlockSpec(memory_space=pltpu.SMEM), whole, whole, whole, whole],
        out_specs=whole,
        out_shape=jax.ShapeDtypeStruct((3, heads, rows), jnp.float32),
        compiler_params=pltpu.CompilerParams(vmem_limit_bytes=VMEM_LIMIT),
        cost_estimate=SMALL,
        name="offsets",
    )(pair_table, by_span, own, near, far)


def attend_kernel(pair_ref, q_ref, cum_ref, *rest, parts, held, scale):
    n_part = len(parts)
    own, crossed, beside, far = (rest[i * n_part : (i + 1) * n_part] for i in range(4))
    out_any, log_ref, near_ref, bias_ref, side_ref, done_ref, in_sems, out_sems = rest[-8:]
    n_ctx = pair_ref.shape[0]
    n, _, rows, size = near_ref.shape
    first = parts[0][0]
    device = lax.axis_index("ctx")
    even = lax.rem(device, 2) == 0
    span = pair_ref[device]
    near_lower = span > pair_ref[lax.rem(device + n_ctx - 1, n_ctx)]
    far_lower = span > pair_ref[lax.rem(device + n_ctx - 2, n_ctx)]

    def store(j, slot):
        return pltpu.make_async_copy(
            done_ref.at[slot], out_any.at[:, first + j, :], out_sems.at[slot]
        )

    for part, (start, count) in enumerate(parts):
        here = pl.ds(start - first, count)

        @pl.when(even)
        def _(part=part, here=here):
            pltpu.make_async_copy(crossed[part], near_ref.at[here], in_sems.at[part]).start()

        @pl.when(jnp.logical_not(even))
        def _(part=part, here=here):
            pltpu.make_async_copy(beside[part], near_ref.at[here], in_sems.at[part]).start()

    side_ref[...] = jnp.zeros_like(side_ref)
    for j in range(n):
        for d in range(3):
            bias_ref[j, d] = cum_ref[d, first + j : first + j + 1, :] * LOG2E
    if held:
        log_ref[...] = rest[4 * n_part + 1][...]

    def one_half(part, k, h, slot, s, pieces):
        sources = (own[part].at[k], near_ref.at[h], far[part].at[k])
        mine = pl.ds(s * HALF, HALF)
        q = q_ref[first + h, 0, mine, :]
        scores = []
        for source, half, masked in pieces:
            block = slice(half * HALF, (half + 1) * HALF)
            prod = lax.dot_general(
                q, sources[source][0, block, :], (((1,), (1,)), ((), ())),
                preferred_element_type=jnp.float32,
            )
            sc = prod * (scale * LOG2E) - bias_ref[h, source, :, block]
            if masked:
                row = lax.broadcasted_iota(jnp.int32, (HALF, HALF), 0)
                col = lax.broadcasted_iota(jnp.int32, (HALF, HALF), 1)
                sc = jnp.where(row >= col, sc, -jnp.inf)
            scores.append(sc)
        top = jnp.max(functools.reduce(jnp.maximum, scores), axis=1, keepdims=True)
        total = acc = None
        for sc, (source, half, _) in zip(scores, pieces):
            block = slice(half * HALF, (half + 1) * HALF)
            w = jnp.exp2(sc - top)
            total = w if total is None else total + w
            o = jnp.dot(
                w.astype(jnp.bfloat16), sources[source][1, block, :],
                preferred_element_type=jnp.float32,
            )
            acc = o if acc is None else acc + o
        total = jnp.sum(total, axis=1, keepdims=True)
        done_ref[slot, mine, :] = acc / total
        lane = lax.broadcasted_iota(jnp.int32, (HALF, size), 1)
        side_ref[mine, :] = jnp.where(lane == h, top + jnp.log2(total), side_ref[mine, :])

    for part, (start, count) in enumerate(parts):
        here = pl.ds(start - first, count)
        pltpu.make_async_copy(crossed[part], near_ref.at[here], in_sems.at[part]).wait()

    for near_is in (False, True):
        for far_is in (False, True):
            lower = [(0, 0, True)]
            upper = [(0, 0, False), (0, 1, True), (1, 0, False), (2, 0, False)]
            (lower if near_is else upper).append((1, 0 if near_is else 1, False))
            (lower if far_is else upper).append((2, 0 if far_is else 1, False))

            @pl.when((near_lower == near_is) & (far_lower == far_is))
            def _(lower=lower, upper=upper):
                for part, (start, count) in enumerate(parts):
                    base = start - first

                    @pl.loop(0, count)
                    def _(k, part=part, base=base):
                        h = base + k
                        slot = lax.rem(h, 2)

                        @pl.when(h >= 2)
                        def _():
                            store(h - 2, slot).wait()

                        one_half(part, k, h, slot, 0, lower)
                        one_half(part, k, h, slot, 1, upper)
                        store(h, slot).start()

    logs = jnp.transpose(side_ref[...])[:n] * (1.0 / LOG2E)
    log_ref[first : first + n, :] = logs + cum_ref[0, first : first + n, :]
    for j in range(max(0, n - 2), n):
        store(j, j % 2).wait()


def attend(parts, pair_table, q, cum, own, crossed, beside, far, previous):
    _, _, rows, size = q.shape
    heads = cum.shape[1]
    n = sum(count for _, count in parts)
    there = pl.BlockSpec(memory_space=pl.ANY)
    whole = pl.BlockSpec(memory_space=pltpu.VMEM)
    args = [pair_table, q, cum, *own, *crossed, *beside, *far]
    in_specs = [pl.BlockSpec(memory_space=pltpu.SMEM)] + [whole] * (2 + 4 * len(parts))
    aliases = {}
    if previous is not None:
        aliases = {len(args): 0, len(args) + 1: 1}
        in_specs += [there, whole]
        args += list(previous)
    return pl.pallas_call(
        functools.partial(
            attend_kernel, parts=parts, held=previous is not None, scale=size**-0.5
        ),
        in_specs=in_specs,
        out_specs=[there, whole],
        out_shape=[
            jax.ShapeDtypeStruct((rows, heads, size), jnp.float32),
            jax.ShapeDtypeStruct((heads, rows), jnp.float32),
        ],
        scratch_shapes=[
            pltpu.VMEM((n, 2, rows, size), jnp.bfloat16),
            pltpu.VMEM((n, 3, 1, rows), jnp.float32),
            pltpu.VMEM((rows, size), jnp.float32),
            pltpu.VMEM((2, rows, size), jnp.float32),
            pltpu.SemaphoreType.DMA((len(parts),)),
            pltpu.SemaphoreType.DMA((2,)),
        ],
        input_output_aliases=aliases,
        compiler_params=pltpu.CompilerParams(vmem_limit_bytes=VMEM_LIMIT),
        cost_estimate=SMALL,
        name="attend",
    )(*args)


def summed_over_ctx(x):
    n_ctx = lax.axis_size("ctx")
    core, column, row, layer = 1, 2, 4, 16

    def behind(x, stride, size, by):
        pairs = []
        for i in range(n_ctx):
            at = i // stride % size
            pairs.append((i, i + ((at - by) % size - at) * stride))
        return lax.ppermute(x, "ctx", pairs)

    both = [(i, i ^ core) for i in range(n_ctx)]
    side = [(i, i ^ column) for i in range(n_ctx)]
    across = [(i, i ^ core ^ column) for i in range(n_ctx)]
    x = x + lax.ppermute(x, "ctx", both) + lax.ppermute(x, "ctx", side) + lax.ppermute(x, "ctx", across)
    x = yield x
    passing = x
    for _ in range(3):
        passing = behind(passing, row, 4, 1)
        x = x + passing
    x = x + behind(x, layer, 8, 1)
    x = x + behind(x, layer, 8, 2)
    passing = behind(behind(x, layer, 8, 2), layer, 8, 2)
    yield x + passing


def shards(tokens, gate_weight, gate_bias, queries, key_vectors, values, pair_table):
    n_ctx = lax.axis_size("ctx")
    next_chip = [(i, (i + (1 if i % 2 else 3)) % n_ctx) for i in range(n_ctx)]
    even_to_odd = [(i, i + 1) for i in range(0, n_ctx, 2)]
    swap = [(i, i ^ 1) for i in range(n_ctx)]
    n_chunk = len(SIZES)

    keep, send = gate_logits(tokens, gate_weight.T)
    recv = lax.ppermute(send, "head", [(0, 1), (1, 0)])
    own = heads_first(SIZES, key_vectors, values, after=(keep,))
    crossed = [lax.ppermute(own[0], "ctx", next_chip)]
    keep, *own = lax.optimization_barrier((keep, *own))
    inner, spread = forget_rows(pair_table, keep, recv, gate_bias)
    steps = summed_over_ctx(spread)
    on_plane = next(steps)
    crossed_inner = lax.ppermute(inner, "ctx", next_chip)
    crossed[0], *own, on_plane, crossed_inner = lax.optimization_barrier(
        (crossed[0], *own, on_plane, crossed_inner)
    )
    for c in range(1, n_chunk):
        crossed.append(lax.ppermute(own[c], "ctx", next_chip))
    beside_inner = lax.ppermute(inner, "ctx", even_to_odd)
    far_inner = lax.ppermute(crossed_inner, "ctx", swap)
    even = lax.rem(lax.axis_index("ctx"), 2) == 0
    near_inner = jnp.where(even, crossed_inner, beside_inner)
    (q,) = heads_first((queries.shape[1],), queries, after=(on_plane,))
    q, on_plane = lax.optimization_barrier((q, on_plane))
    by_span = steps.send(on_plane)
    cum = offsets(pair_table, by_span, inner, near_inner, far_inner)
    starts = [sum(SIZES[:c]) for c in range(n_chunk)]
    beside = [None] * n_chunk
    far = [None] * n_chunk
    results = earlier = None
    for group in GROUPS:
        for c in group:
            gate = earlier if group == GROUPS[-1] else results
            mine, gate = lax.optimization_barrier((own[c], gate))
            beside[c] = lax.ppermute(mine, "ctx", even_to_odd)
            across, results = lax.optimization_barrier((crossed[c], results))
            far[c] = lax.ppermute(across, "ctx", swap)
        earlier = results
        results = attend(
            tuple((starts[c], SIZES[c]) for c in group), pair_table, q, cum,
            [own[c] for c in group], [crossed[c] for c in group],
            [beside[c] for c in group], [far[c] for c in group], results,
        )
    out, log_total = results
    return out, log_total.T


def solution(mesh):
    return jax.shard_map(
        shards,
        mesh=mesh,
        in_specs=(
            P("ctx", "head"),
            P("head", None),
            P("head"),
            P("ctx", "head", None),
            P("ctx", "head", None),
            P("ctx", "head", None),
            P(),
        ),
        out_specs=(P("ctx", "head", None), P("ctx", "head")),
        check_vma=False,
    )
```

```python
import functools
import math

import jax
import jax.numpy as jnp
from jax import lax
from jax.experimental import pallas as pl
from jax.experimental.pallas import tpu as pltpu
from jax.sharding import PartitionSpec as P

VMEM_LIMIT = 24 * 1024 * 1024
HALF = 256
SIZES = (1, 4, 4, 5, 2)
GROUPS = ((0,), (1, 2), (3,), (4,))
LOG2E = math.log2(math.e)


SMALL = pl.CostEstimate(flops=1, bytes_accessed=1, transcendentals=0)


def gate_kernel(tok_ref, w_ref, keep_ref, send_ref):
    logits = lax.dot_general(
        tok_ref[...], w_ref[...], (((1,), (1,)), ((), ())), preferred_element_type=jnp.float32
    )
    logits = jnp.transpose(logits)
    heads = keep_ref.shape[0]
    first = lax.axis_index("head") == 0
    low, high = logits[:heads], logits[heads:]
    keep_ref[...] = jnp.where(first, low, high)
    send_ref[...] = jnp.where(first, high, low)


def gate_logits(tokens, gate_weight):
    rows, depth = tokens.shape
    heads = gate_weight.shape[0] // 2
    step = 256
    out = jax.ShapeDtypeStruct((heads, rows), jnp.float32)
    return pl.pallas_call(
        gate_kernel,
        grid=(rows // step,),
        in_specs=[
            pl.BlockSpec((step, depth), lambda i: (i, 0)),
            pl.BlockSpec(gate_weight.shape, lambda i: (0, 0)),
        ],
        out_specs=[pl.BlockSpec((heads, step), lambda i: (0, i))] * 2,
        out_shape=[out, out],
        compiler_params=pltpu.CompilerParams(vmem_limit_bytes=VMEM_LIMIT),
        cost_estimate=SMALL,
        name="gate_logits",
    )(tokens, gate_weight)


def heads_first_kernel(*refs, n_in, sizes):
    ins, outs = refs[:n_in], refs[-len(sizes) :]
    for which, ref in enumerate(ins):
        turned = jnp.swapaxes(ref[...], 0, 1)
        first = 0
        for out, n in zip(outs, sizes):
            out[:, which] = turned[first : first + n]
            first += n


def heads_first(sizes, *arrays, after=()):
    rows, heads, size = arrays[0].shape
    step = 128
    n_in = len(arrays)
    return pl.pallas_call(
        functools.partial(heads_first_kernel, n_in=n_in, sizes=sizes),
        grid=(rows // step,),
        in_specs=[pl.BlockSpec((step, heads, size), lambda i: (i, 0, 0))] * n_in
        + [pl.BlockSpec(memory_space=pl.ANY)] * len(after),
        out_specs=[pl.BlockSpec((n, n_in, step, size), lambda i: (0, 0, i, 0)) for n in sizes],
        out_shape=[jax.ShapeDtypeStruct((n, n_in, rows, size), jnp.bfloat16) for n in sizes],
        compiler_params=pltpu.CompilerParams(vmem_limit_bytes=VMEM_LIMIT),
        cost_estimate=SMALL,
        name="heads_first",
    )(*arrays, *after)


def forget_kernel(pair_ref, keep_ref, recv_ref, bias_ref, inner_ref, spread_ref):
    device = lax.axis_index("ctx")
    n_span = 2 * pair_ref.shape[0]
    line = lax.broadcasted_iota(jnp.int32, keep_ref.shape, 0)
    bias = jnp.zeros(keep_ref.shape, jnp.float32)
    for h in range(keep_ref.shape[0]):
        bias = jnp.where(line == h, bias_ref[h], bias)
    logits = keep_ref[...] + recv_ref[...] + bias
    forget = (jnp.minimum(logits, 0.0) - jnp.log1p(jnp.exp(-jnp.abs(logits)))).astype(jnp.bfloat16)
    row = lax.broadcasted_iota(jnp.int32, (HALF, HALF), 0)
    col = lax.broadcasted_iota(jnp.int32, (HALF, HALF), 1)
    upto = (row <= col).astype(jnp.float32).astype(jnp.bfloat16)
    low = jnp.dot(forget[:, :HALF], upto, preferred_element_type=jnp.float32)
    high = jnp.dot(forget[:, HALF:], upto, preferred_element_type=jnp.float32)
    inner_ref[:, :HALF] = low
    inner_ref[:, HALF:] = high
    span = pair_ref[device]
    lane = lax.broadcasted_iota(jnp.int32, spread_ref.shape, 1)
    spread_ref[...] = jnp.where(lane == span, low[:, HALF - 1 :], 0.0) + jnp.where(
        lane == n_span - 1 - span, high[:, HALF - 1 :], 0.0
    )


def forget_rows(pair_table, keep, recv, bias):
    heads, rows = keep.shape
    n_span = 2 * pair_table.shape[0]
    whole = pl.BlockSpec(memory_space=pltpu.VMEM)
    return pl.pallas_call(
        forget_kernel,
        in_specs=[
            pl.BlockSpec(memory_space=pltpu.SMEM),
            whole,
            whole,
            pl.BlockSpec(memory_space=pltpu.SMEM),
        ],
        out_specs=[whole, whole],
        out_shape=[
            jax.ShapeDtypeStruct((heads, rows), jnp.float32),
            jax.ShapeDtypeStruct((heads, n_span), jnp.float32),
        ],
        compiler_params=pltpu.CompilerParams(vmem_limit_bytes=VMEM_LIMIT),
        cost_estimate=SMALL,
        name="forget_rows",
    )(pair_table, keep, recv, bias)


def offsets_kernel(pair_ref, by_span_ref, own_ref, near_ref, far_ref, cum_ref):
    n_ctx = pair_ref.shape[0]
    device = lax.axis_index("ctx")
    by_span = by_span_ref[...]
    lane = lax.broadcasted_iota(jnp.int32, by_span.shape, 1)
    for distance, ref in enumerate((own_ref, near_ref, far_ref)):
        span = pair_ref[lax.rem(device + n_ctx - distance, n_ctx)]
        for s, c in enumerate((span, 2 * n_ctx - 1 - span)):
            offset = jnp.sum(jnp.where(lane < c, by_span, 0.0), axis=1, keepdims=True)
            part = slice(s * HALF, (s + 1) * HALF)
            cum_ref[distance, :, part] = ref[:, part] + offset


def offsets(pair_table, by_span, own, near, far):
    heads, rows = own.shape
    whole = pl.BlockSpec(memory_space=pltpu.VMEM)
    return pl.pallas_call(
        offsets_kernel,
        in_specs=[pl.BlockSpec(memory_space=pltpu.SMEM), whole, whole, whole, whole],
        out_specs=whole,
        out_shape=jax.ShapeDtypeStruct((3, heads, rows), jnp.float32),
        compiler_params=pltpu.CompilerParams(vmem_limit_bytes=VMEM_LIMIT),
        cost_estimate=SMALL,
        name="offsets",
    )(pair_table, by_span, own, near, far)


def attend_kernel(pair_ref, q_ref, cum_ref, *rest, parts, held, scale):
    n_part = len(parts)
    own, crossed, beside, far = (rest[i * n_part : (i + 1) * n_part] for i in range(4))
    out_any, log_ref, near_ref, bias_ref, side_ref, done_ref, in_sems, out_sems = rest[-8:]
    n_ctx = pair_ref.shape[0]
    n, _, rows, size = near_ref.shape
    first = parts[0][0]
    device = lax.axis_index("ctx")
    even = lax.rem(device, 2) == 0
    span = pair_ref[device]
    near_lower = span > pair_ref[lax.rem(device + n_ctx - 1, n_ctx)]
    far_lower = span > pair_ref[lax.rem(device + n_ctx - 2, n_ctx)]

    def store(j, slot):
        return pltpu.make_async_copy(
            done_ref.at[slot], out_any.at[:, first + j, :], out_sems.at[slot]
        )

    for part, (start, count) in enumerate(parts):
        here = pl.ds(start - first, count)

        @pl.when(even)
        def _(part=part, here=here):
            pltpu.make_async_copy(crossed[part], near_ref.at[here], in_sems.at[part]).start()

        @pl.when(jnp.logical_not(even))
        def _(part=part, here=here):
            pltpu.make_async_copy(beside[part], near_ref.at[here], in_sems.at[part]).start()

    side_ref[...] = jnp.zeros_like(side_ref)
    for j in range(n):
        for d in range(3):
            bias_ref[j, d] = cum_ref[d, first + j : first + j + 1, :] * LOG2E
    if held:
        log_ref[...] = rest[4 * n_part + 1][...]

    def one_half(part, k, h, slot, s, pieces):
        sources = (own[part].at[k], near_ref.at[h], far[part].at[k])
        mine = pl.ds(s * HALF, HALF)
        q = q_ref[first + h, 0, mine, :]
        scores = []
        for source, half, masked in pieces:
            block = slice(half * HALF, (half + 1) * HALF)
            prod = lax.dot_general(
                q, sources[source][0, block, :], (((1,), (1,)), ((), ())),
                preferred_element_type=jnp.float32,
            )
            sc = prod * (scale * LOG2E) - bias_ref[h, source, :, block]
            if masked:
                row = lax.broadcasted_iota(jnp.int32, (HALF, HALF), 0)
                col = lax.broadcasted_iota(jnp.int32, (HALF, HALF), 1)
                sc = jnp.where(row >= col, sc, -jnp.inf)
            scores.append(sc)
        top = jnp.max(functools.reduce(jnp.maximum, scores), axis=1, keepdims=True)
        total = acc = None
        for sc, (source, half, _) in zip(scores, pieces):
            block = slice(half * HALF, (half + 1) * HALF)
            w = jnp.exp2(sc - top)
            total = w if total is None else total + w
            o = jnp.dot(
                w.astype(jnp.bfloat16), sources[source][1, block, :],
                preferred_element_type=jnp.float32,
            )
            acc = o if acc is None else acc + o
        total = jnp.sum(total, axis=1, keepdims=True)
        done_ref[slot, mine, :] = acc / total
        lane = lax.broadcasted_iota(jnp.int32, (HALF, size), 1)
        side_ref[mine, :] = jnp.where(lane == h, top + jnp.log2(total), side_ref[mine, :])

    for part, (start, count) in enumerate(parts):
        here = pl.ds(start - first, count)
        pltpu.make_async_copy(crossed[part], near_ref.at[here], in_sems.at[part]).wait()

    for near_is in (False, True):
        for far_is in (False, True):
            lower = [(0, 0, True)]
            upper = [(0, 0, False), (0, 1, True), (1, 0, False), (2, 0, False)]
            (lower if near_is else upper).append((1, 0 if near_is else 1, False))
            (lower if far_is else upper).append((2, 0 if far_is else 1, False))

            @pl.when((near_lower == near_is) & (far_lower == far_is))
            def _(lower=lower, upper=upper):
                for part, (start, count) in enumerate(parts):
                    base = start - first

                    @pl.loop(0, count)
                    def _(k, part=part, base=base):
                        h = base + k
                        slot = lax.rem(h, 2)

                        @pl.when(h >= 2)
                        def _():
                            store(h - 2, slot).wait()

                        one_half(part, k, h, slot, 0, lower)
                        one_half(part, k, h, slot, 1, upper)
                        store(h, slot).start()

    logs = jnp.transpose(side_ref[...])[:n] * (1.0 / LOG2E)
    log_ref[first : first + n, :] = logs + cum_ref[0, first : first + n, :]
    for j in range(max(0, n - 2), n):
        store(j, j % 2).wait()


def attend(parts, pair_table, q, cum, own, crossed, beside, far, previous):
    _, _, rows, size = q.shape
    heads = cum.shape[1]
    n = sum(count for _, count in parts)
    there = pl.BlockSpec(memory_space=pl.ANY)
    whole = pl.BlockSpec(memory_space=pltpu.VMEM)
    args = [pair_table, q, cum, *own, *crossed, *beside, *far]
    in_specs = [pl.BlockSpec(memory_space=pltpu.SMEM)] + [whole] * (2 + 4 * len(parts))
    aliases = {}
    if previous is not None:
        aliases = {len(args): 0, len(args) + 1: 1}
        in_specs += [there, whole]
        args += list(previous)
    return pl.pallas_call(
        functools.partial(
            attend_kernel, parts=parts, held=previous is not None, scale=size**-0.5
        ),
        in_specs=in_specs,
        out_specs=[there, whole],
        out_shape=[
            jax.ShapeDtypeStruct((rows, heads, size), jnp.float32),
            jax.ShapeDtypeStruct((heads, rows), jnp.float32),
        ],
        scratch_shapes=[
            pltpu.VMEM((n, 2, rows, size), jnp.bfloat16),
            pltpu.VMEM((n, 3, 1, rows), jnp.float32),
            pltpu.VMEM((rows, size), jnp.float32),
            pltpu.VMEM((2, rows, size), jnp.float32),
            pltpu.SemaphoreType.DMA((len(parts),)),
            pltpu.SemaphoreType.DMA((2,)),
        ],
        input_output_aliases=aliases,
        compiler_params=pltpu.CompilerParams(vmem_limit_bytes=VMEM_LIMIT),
        cost_estimate=SMALL,
        name="attend",
    )(*args)


def summed_over_ctx(x):
    n_ctx = lax.axis_size("ctx")
    core, column, row, layer = 1, 2, 4, 16

    def behind(x, stride, size, by):
        pairs = []
        for i in range(n_ctx):
            at = i // stride % size
            pairs.append((i, i + ((at - by) % size - at) * stride))
        return lax.ppermute(x, "ctx", pairs)

    both = [(i, i ^ core) for i in range(n_ctx)]
    side = [(i, i ^ column) for i in range(n_ctx)]
    across = [(i, i ^ core ^ column) for i in range(n_ctx)]
    x = x + lax.ppermute(x, "ctx", both) + lax.ppermute(x, "ctx", side) + lax.ppermute(x, "ctx", across)
    x = yield x
    passing = x
    for _ in range(3):
        passing = behind(passing, row, 4, 1)
        x = x + passing
    x = x + behind(x, layer, 8, 1)
    x = x + behind(x, layer, 8, 2)
    passing = behind(behind(x, layer, 8, 2), layer, 8, 2)
    yield x + passing


def shards(tokens, gate_weight, gate_bias, queries, key_vectors, values, pair_table):
    n_ctx = lax.axis_size("ctx")
    next_chip = [(i, (i + (1 if i % 2 else 3)) % n_ctx) for i in range(n_ctx)]
    even_to_odd = [(i, i + 1) for i in range(0, n_ctx, 2)]
    swap = [(i, i ^ 1) for i in range(n_ctx)]
    n_chunk = len(SIZES)

    keep, send = gate_logits(tokens, gate_weight.T)
    recv = lax.ppermute(send, "head", [(0, 1), (1, 0)])
    own = heads_first(SIZES, key_vectors, values, after=(keep,))
    crossed = [lax.ppermute(own[0], "ctx", next_chip)]
    keep, *own = lax.optimization_barrier((keep, *own))
    inner, spread = forget_rows(pair_table, keep, recv, gate_bias)
    steps = summed_over_ctx(spread)
    on_plane = next(steps)
    crossed_inner = lax.ppermute(inner, "ctx", next_chip)
    *own, on_plane = lax.optimization_barrier((*own, on_plane))
    crossed[0], *later, crossed_inner = lax.optimization_barrier(
        (crossed[0], *own[2:], crossed_inner)
    )
    own = [*own[:2], *later]
    for c in range(1, n_chunk):
        crossed.append(lax.ppermute(own[c], "ctx", next_chip))
    beside_inner = lax.ppermute(inner, "ctx", even_to_odd)
    far_inner = lax.ppermute(crossed_inner, "ctx", swap)
    even = lax.rem(lax.axis_index("ctx"), 2) == 0
    near_inner = jnp.where(even, crossed_inner, beside_inner)
    (q,) = heads_first((queries.shape[1],), queries, after=(on_plane,))
    q, on_plane = lax.optimization_barrier((q, on_plane))
    by_span = steps.send(on_plane)
    cum = offsets(pair_table, by_span, inner, near_inner, far_inner)
    starts = [sum(SIZES[:c]) for c in range(n_chunk)]
    beside = [None] * n_chunk
    far = [None] * n_chunk
    results = earlier = None
    for group in GROUPS:
        for c in group:
            gate = earlier if group == GROUPS[-1] else results
            mine, gate = lax.optimization_barrier((own[c], gate))
            beside[c] = lax.ppermute(mine, "ctx", even_to_odd)
            across, results = lax.optimization_barrier((crossed[c], results))
            far[c] = lax.ppermute(across, "ctx", swap)
        earlier = results
        results = attend(
            tuple((starts[c], SIZES[c]) for c in group), pair_table, q, cum,
            [own[c] for c in group], [crossed[c] for c in group],
            [beside[c] for c in group], [far[c] for c in group], results,
        )
    out, log_total = results
    return out, log_total.T


def solution(mesh):
    return jax.shard_map(
        shards,
        mesh=mesh,
        in_specs=(
            P("ctx", "head"),
            P("head", None),
            P("head"),
            P("ctx", "head", None),
            P("ctx", "head", None),
            P("ctx", "head", None),
            P(),
        ),
        out_specs=(P("ctx", "head", None), P("ctx", "head")),
        check_vma=False,
    )
```

```python
import functools
import math

import jax
import jax.numpy as jnp
from jax import lax
from jax.experimental import pallas as pl
from jax.experimental.pallas import tpu as pltpu
from jax.sharding import PartitionSpec as P

VMEM_LIMIT = 24 * 1024 * 1024
HALF = 256
SIZES = (1, 4, 4, 5, 2)
GROUPS = ((0,), (1, 2), (3,), (4,))
LOG2E = math.log2(math.e)


SMALL = pl.CostEstimate(flops=1, bytes_accessed=1, transcendentals=0)


def gate_kernel(tok_ref, w_ref, keep_ref, send_ref):
    logits = lax.dot_general(
        tok_ref[...], w_ref[...], (((1,), (1,)), ((), ())), preferred_element_type=jnp.float32
    )
    logits = jnp.transpose(logits)
    heads = keep_ref.shape[0]
    first = lax.axis_index("head") == 0
    low, high = logits[:heads], logits[heads:]
    keep_ref[...] = jnp.where(first, low, high)
    send_ref[...] = jnp.where(first, high, low)


def gate_logits(tokens, gate_weight):
    rows, depth = tokens.shape
    heads = gate_weight.shape[0] // 2
    step = 256
    out = jax.ShapeDtypeStruct((heads, rows), jnp.float32)
    return pl.pallas_call(
        gate_kernel,
        grid=(rows // step,),
        in_specs=[
            pl.BlockSpec((step, depth), lambda i: (i, 0)),
            pl.BlockSpec(gate_weight.shape, lambda i: (0, 0)),
        ],
        out_specs=[pl.BlockSpec((heads, step), lambda i: (0, i))] * 2,
        out_shape=[out, out],
        compiler_params=pltpu.CompilerParams(vmem_limit_bytes=56 * 1024 * 1024),
        cost_estimate=SMALL,
        name="gate_logits",
    )(tokens, gate_weight)


def heads_first_kernel(*refs, n_in, sizes):
    ins, outs = refs[:n_in], refs[-len(sizes) :]
    for which, ref in enumerate(ins):
        turned = jnp.swapaxes(ref[...], 0, 1)
        first = 0
        for out, n in zip(outs, sizes):
            out[:, which] = turned[first : first + n]
            first += n


def heads_first(sizes, *arrays, after=()):
    rows, heads, size = arrays[0].shape
    step = 128
    n_in = len(arrays)
    return pl.pallas_call(
        functools.partial(heads_first_kernel, n_in=n_in, sizes=sizes),
        grid=(rows // step,),
        in_specs=[pl.BlockSpec((step, heads, size), lambda i: (i, 0, 0))] * n_in
        + [pl.BlockSpec(memory_space=pl.ANY)] * len(after),
        out_specs=[pl.BlockSpec((n, n_in, step, size), lambda i: (0, 0, i, 0)) for n in sizes],
        out_shape=[jax.ShapeDtypeStruct((n, n_in, rows, size), jnp.bfloat16) for n in sizes],
        compiler_params=pltpu.CompilerParams(vmem_limit_bytes=VMEM_LIMIT),
        cost_estimate=SMALL,
        name="heads_first",
    )(*arrays, *after)


def forget_kernel(pair_ref, keep_ref, recv_ref, bias_ref, inner_ref, spread_ref):
    device = lax.axis_index("ctx")
    n_span = 2 * pair_ref.shape[0]
    line = lax.broadcasted_iota(jnp.int32, keep_ref.shape, 0)
    bias = jnp.zeros(keep_ref.shape, jnp.float32)
    for h in range(keep_ref.shape[0]):
        bias = jnp.where(line == h, bias_ref[h], bias)
    logits = keep_ref[...] + recv_ref[...] + bias
    forget = (jnp.minimum(logits, 0.0) - jnp.log1p(jnp.exp(-jnp.abs(logits)))).astype(jnp.bfloat16)
    row = lax.broadcasted_iota(jnp.int32, (HALF, HALF), 0)
    col = lax.broadcasted_iota(jnp.int32, (HALF, HALF), 1)
    upto = (row <= col).astype(jnp.float32).astype(jnp.bfloat16)
    low = jnp.dot(forget[:, :HALF], upto, preferred_element_type=jnp.float32)
    high = jnp.dot(forget[:, HALF:], upto, preferred_element_type=jnp.float32)
    inner_ref[:, :HALF] = low
    inner_ref[:, HALF:] = high
    span = pair_ref[device]
    lane = lax.broadcasted_iota(jnp.int32, spread_ref.shape, 1)
    spread_ref[...] = jnp.where(lane == span, low[:, HALF - 1 :], 0.0) + jnp.where(
        lane == n_span - 1 - span, high[:, HALF - 1 :], 0.0
    )


def forget_rows(pair_table, keep, recv, bias):
    heads, rows = keep.shape
    n_span = 2 * pair_table.shape[0]
    whole = pl.BlockSpec(memory_space=pltpu.VMEM)
    return pl.pallas_call(
        forget_kernel,
        in_specs=[
            pl.BlockSpec(memory_space=pltpu.SMEM),
            whole,
            whole,
            pl.BlockSpec(memory_space=pltpu.SMEM),
        ],
        out_specs=[whole, whole],
        out_shape=[
            jax.ShapeDtypeStruct((heads, rows), jnp.float32),
            jax.ShapeDtypeStruct((heads, n_span), jnp.float32),
        ],
        compiler_params=pltpu.CompilerParams(vmem_limit_bytes=VMEM_LIMIT),
        cost_estimate=SMALL,
        name="forget_rows",
    )(pair_table, keep, recv, bias)


def offsets_kernel(pair_ref, by_span_ref, own_ref, near_ref, far_ref, cum_ref):
    n_ctx = pair_ref.shape[0]
    device = lax.axis_index("ctx")
    by_span = by_span_ref[...]
    lane = lax.broadcasted_iota(jnp.int32, by_span.shape, 1)
    for distance, ref in enumerate((own_ref, near_ref, far_ref)):
        span = pair_ref[lax.rem(device + n_ctx - distance, n_ctx)]
        for s, c in enumerate((span, 2 * n_ctx - 1 - span)):
            offset = jnp.sum(jnp.where(lane < c, by_span, 0.0), axis=1, keepdims=True)
            part = slice(s * HALF, (s + 1) * HALF)
            cum_ref[distance, :, part] = ref[:, part] + offset


def offsets(pair_table, by_span, own, near, far):
    heads, rows = own.shape
    whole = pl.BlockSpec(memory_space=pltpu.VMEM)
    return pl.pallas_call(
        offsets_kernel,
        in_specs=[pl.BlockSpec(memory_space=pltpu.SMEM), whole, whole, whole, whole],
        out_specs=whole,
        out_shape=jax.ShapeDtypeStruct((3, heads, rows), jnp.float32),
        compiler_params=pltpu.CompilerParams(vmem_limit_bytes=VMEM_LIMIT),
        cost_estimate=SMALL,
        name="offsets",
    )(pair_table, by_span, own, near, far)


def attend_kernel(pair_ref, q_ref, cum_ref, *rest, parts, held, scale):
    n_part = len(parts)
    own, crossed, beside, far = (rest[i * n_part : (i + 1) * n_part] for i in range(4))
    out_any, log_ref, near_ref, bias_ref, side_ref, done_ref, in_sems, out_sems = rest[-8:]
    n_ctx = pair_ref.shape[0]
    n, _, rows, size = near_ref.shape
    first = parts[0][0]
    device = lax.axis_index("ctx")
    even = lax.rem(device, 2) == 0
    span = pair_ref[device]
    near_lower = span > pair_ref[lax.rem(device + n_ctx - 1, n_ctx)]
    far_lower = span > pair_ref[lax.rem(device + n_ctx - 2, n_ctx)]

    def store(j, slot):
        return pltpu.make_async_copy(
            done_ref.at[slot], out_any.at[:, first + j, :], out_sems.at[slot]
        )

    for part, (start, count) in enumerate(parts):
        here = pl.ds(start - first, count)

        @pl.when(even)
        def _(part=part, here=here):
            pltpu.make_async_copy(crossed[part], near_ref.at[here], in_sems.at[part]).start()

        @pl.when(jnp.logical_not(even))
        def _(part=part, here=here):
            pltpu.make_async_copy(beside[part], near_ref.at[here], in_sems.at[part]).start()

    side_ref[...] = jnp.zeros_like(side_ref)
    for j in range(n):
        for d in range(3):
            bias_ref[j, d] = cum_ref[d, first + j : first + j + 1, :] * LOG2E
    if held:
        log_ref[...] = rest[4 * n_part + 1][...]

    def one_half(part, k, h, slot, s, pieces):
        sources = (own[part].at[k], near_ref.at[h], far[part].at[k])
        mine = pl.ds(s * HALF, HALF)
        q = q_ref[first + h, 0, mine, :]
        scores = []
        for source, half, masked in pieces:
            block = slice(half * HALF, (half + 1) * HALF)
            prod = lax.dot_general(
                q, sources[source][0, block, :], (((1,), (1,)), ((), ())),
                preferred_element_type=jnp.float32,
            )
            sc = prod * (scale * LOG2E) - bias_ref[h, source, :, block]
            if masked:
                row = lax.broadcasted_iota(jnp.int32, (HALF, HALF), 0)
                col = lax.broadcasted_iota(jnp.int32, (HALF, HALF), 1)
                sc = jnp.where(row >= col, sc, -jnp.inf)
            scores.append(sc)
        top = jnp.max(functools.reduce(jnp.maximum, scores), axis=1, keepdims=True)
        total = acc = None
        for sc, (source, half, _) in zip(scores, pieces):
            block = slice(half * HALF, (half + 1) * HALF)
            w = jnp.exp2(sc - top)
            total = w if total is None else total + w
            o = jnp.dot(
                w.astype(jnp.bfloat16), sources[source][1, block, :],
                preferred_element_type=jnp.float32,
            )
            acc = o if acc is None else acc + o
        total = jnp.sum(total, axis=1, keepdims=True)
        done_ref[slot, mine, :] = acc / total
        lane = lax.broadcasted_iota(jnp.int32, (HALF, size), 1)
        side_ref[mine, :] = jnp.where(lane == h, top + jnp.log2(total), side_ref[mine, :])

    for part, (start, count) in enumerate(parts):
        here = pl.ds(start - first, count)
        pltpu.make_async_copy(crossed[part], near_ref.at[here], in_sems.at[part]).wait()

    for near_is in (False, True):
        for far_is in (False, True):
            lower = [(0, 0, True)]
            upper = [(0, 0, False), (0, 1, True), (1, 0, False), (2, 0, False)]
            (lower if near_is else upper).append((1, 0 if near_is else 1, False))
            (lower if far_is else upper).append((2, 0 if far_is else 1, False))

            @pl.when((near_lower == near_is) & (far_lower == far_is))
            def _(lower=lower, upper=upper):
                for part, (start, count) in enumerate(parts):
                    base = start - first

                    @pl.loop(0, count)
                    def _(k, part=part, base=base):
                        h = base + k
                        slot = lax.rem(h, 2)

                        @pl.when(h >= 2)
                        def _():
                            store(h - 2, slot).wait()

                        one_half(part, k, h, slot, 0, lower)
                        one_half(part, k, h, slot, 1, upper)
                        store(h, slot).start()

    logs = jnp.transpose(side_ref[...])[:n] * (1.0 / LOG2E)
    log_ref[first : first + n, :] = logs
    for j in range(max(0, n - 2), n):
        store(j, j % 2).wait()


def attend(parts, pair_table, q, cum, own, crossed, beside, far, previous):
    _, _, rows, size = q.shape
    heads = cum.shape[1]
    n = sum(count for _, count in parts)
    there = pl.BlockSpec(memory_space=pl.ANY)
    whole = pl.BlockSpec(memory_space=pltpu.VMEM)
    args = [pair_table, q, cum, *own, *crossed, *beside, *far]
    in_specs = [pl.BlockSpec(memory_space=pltpu.SMEM)] + [whole] * (2 + 4 * len(parts))
    aliases = {}
    if previous is not None:
        aliases = {len(args): 0, len(args) + 1: 1}
        in_specs += [there, whole]
        args += list(previous)
    return pl.pallas_call(
        functools.partial(
            attend_kernel, parts=parts, held=previous is not None, scale=size**-0.5
        ),
        in_specs=in_specs,
        out_specs=[there, whole],
        out_shape=[
            jax.ShapeDtypeStruct((rows, heads, size), jnp.float32),
            jax.ShapeDtypeStruct((heads, rows), jnp.float32),
        ],
        scratch_shapes=[
            pltpu.VMEM((n, 2, rows, size), jnp.bfloat16),
            pltpu.VMEM((n, 3, 1, rows), jnp.float32),
            pltpu.VMEM((rows, size), jnp.float32),
            pltpu.VMEM((2, rows, size), jnp.float32),
            pltpu.SemaphoreType.DMA((len(parts),)),
            pltpu.SemaphoreType.DMA((2,)),
        ],
        input_output_aliases=aliases,
        compiler_params=pltpu.CompilerParams(vmem_limit_bytes=VMEM_LIMIT),
        cost_estimate=SMALL,
        name="attend",
    )(*args)


def summed_over_ctx(x):
    n_ctx = lax.axis_size("ctx")
    core, column, row, layer = 1, 2, 4, 16

    def behind(x, stride, size, by):
        pairs = []
        for i in range(n_ctx):
            at = i // stride % size
            pairs.append((i, i + ((at - by) % size - at) * stride))
        return lax.ppermute(x, "ctx", pairs)

    both = [(i, i ^ core) for i in range(n_ctx)]
    side = [(i, i ^ column) for i in range(n_ctx)]
    across = [(i, i ^ core ^ column) for i in range(n_ctx)]
    x = x + lax.ppermute(x, "ctx", both) + lax.ppermute(x, "ctx", side) + lax.ppermute(x, "ctx", across)
    x = yield x
    passing = x
    for _ in range(3):
        passing = behind(passing, row, 4, 1)
        x = x + passing
    x = x + behind(x, layer, 8, 1)
    x = x + behind(x, layer, 8, 2)
    passing = behind(behind(x, layer, 8, 2), layer, 8, 2)
    yield x + passing


def shards(tokens, gate_weight, gate_bias, queries, key_vectors, values, pair_table):
    n_ctx = lax.axis_size("ctx")
    next_chip = [(i, (i + (1 if i % 2 else 3)) % n_ctx) for i in range(n_ctx)]
    even_to_odd = [(i, i + 1) for i in range(0, n_ctx, 2)]
    swap = [(i, i ^ 1) for i in range(n_ctx)]
    n_chunk = len(SIZES)

    keep, send = gate_logits(tokens, gate_weight.T)
    recv = lax.ppermute(send, "head", [(0, 1), (1, 0)])
    own = heads_first(SIZES, key_vectors, values, after=(keep,))
    crossed = [lax.ppermute(own[0], "ctx", next_chip)]
    keep, *own = lax.optimization_barrier((keep, *own))
    inner, spread = forget_rows(pair_table, keep, recv, gate_bias)
    steps = summed_over_ctx(spread)
    on_plane = next(steps)
    crossed_inner = lax.ppermute(inner, "ctx", next_chip)
    *own, on_plane = lax.optimization_barrier((*own, on_plane))
    crossed[0], *later, crossed_inner = lax.optimization_barrier(
        (crossed[0], *own[2:], crossed_inner)
    )
    own = [*own[:2], *later]
    for c in range(1, n_chunk):
        crossed.append(lax.ppermute(own[c], "ctx", next_chip))
    beside_inner = lax.ppermute(inner, "ctx", even_to_odd)
    far_inner = lax.ppermute(crossed_inner, "ctx", swap)
    even = lax.rem(lax.axis_index("ctx"), 2) == 0
    near_inner = jnp.where(even, crossed_inner, beside_inner)
    (q,) = heads_first((queries.shape[1],), queries, after=(on_plane,))
    q, on_plane = lax.optimization_barrier((q, on_plane))
    by_span = steps.send(on_plane)
    cum = offsets(pair_table, by_span, inner, near_inner, far_inner)
    starts = [sum(SIZES[:c]) for c in range(n_chunk)]
    beside = [None] * n_chunk
    far = [None] * n_chunk
    results = earlier = None
    for group in GROUPS:
        for c in group:
            gate = earlier if group == GROUPS[-1] else results
            mine, gate = lax.optimization_barrier((own[c], gate))
            beside[c] = lax.ppermute(mine, "ctx", even_to_odd)
            across, results = lax.optimization_barrier((crossed[c], results))
            far[c] = lax.ppermute(across, "ctx", swap)
        earlier = results
        results = attend(
            tuple((starts[c], SIZES[c]) for c in group), pair_table, q, cum,
            [own[c] for c in group], [crossed[c] for c in group],
            [beside[c] for c in group], [far[c] for c in group], results,
        )
    out, log_total = results
    return out, (log_total + cum[0]).T


def solution(mesh):
    return jax.shard_map(
        shards,
        mesh=mesh,
        in_specs=(
            P("ctx", "head"),
            P("head", None),
            P("head"),
            P("ctx", "head", None),
            P("ctx", "head", None),
            P("ctx", "head", None),
            P(),
        ),
        out_specs=(P("ctx", "head", None), P("ctx", "head")),
        check_vma=False,
    )
```
